512 devices in a mesh: dp: 16 (over z), pts: 32 (over x, y, core).
Axes of the slice: x: 4, y: 4, z: 16, core: 2. Of those that a mesh axis runs over, the one named last changes fastest.
Arguments:
- x_mid: bfloat16 [98304, 1024], P(('dp', 'pts')), parts along dimension 0, may hold values from -30 to 30
- fx_mid: bfloat16 [98304, 1024], P(('dp', 'pts')), parts along dimension 0, may hold values from -20 to 20
- gumbel: bfloat16 [98304, 8192], P(('dp', 'pts')), parts along dimension 0, may hold values from -2.5 to 240
- w_slice: bfloat16 [64, 512], replicated, may hold values from -0.75 to 0.75
- w_temp: bfloat16 [64], replicated, may hold values from -0.75 to 0.75
- query_weight: float32 [64, 64], replicated, may hold values from -12 to 12
- key_weight: float32 [64, 64], replicated, may hold values from -12 to 12
- value_weight: float32 [64, 64], replicated, may hold values from -1.5 to 1.5
Outputs:
- sliced_out: bfloat16 [98304, 1024], P(('dp', 'pts')), parts along dimension 0
The draws below stay inside these ranges and needn't reach their ends.
There are 16 independent parts, one for each index of `dp`. The reference program is written for one: setup_inputs(seed, part) draws one part's arguments, and reference() takes and returns one part's arrays. A program takes and returns all parts, laid end to end along the dimension named above; an argument that names none is the same for every part. Nothing has to cross between parts.
All inputs are finite; a program needn't handle non-finite values.
Results may differ from the reference program's by a relative error of at most 0.0065.
The reference program's roundings to bfloat16 on the way count: a program that leaves them out, or rounds other values in their place, can miss the bound.
Values may be sent and summed in bfloat16 or wider, within the bound.
No kernel may reach another device: no remote copies, remote signals or barrier semaphores. Data moves between devices by JAX's collectives and lax.ppermute only.
A program may use at most 64 MiB of HBM per device.

```python
import math
import jax
import jax.numpy as jnp
from jax import lax

H = 16
DH = 64
M = 512
PTS_DEV = 192
POINTS = 6144


def draw_query_weight(key, part):
    key = jax.random.fold_in(key, 31)
    return jnp.clip(0.7 * jax.random.normal(key, (DH, DH), jnp.float32), -12.0, 12.0)


def draw_key_weight(key, part):
    key = jax.random.fold_in(key, 37)
    return jnp.clip(0.7 * jax.random.normal(key, (DH, DH), jnp.float32), -12.0, 12.0)


def draw_x_mid(key, part):
    key = jax.random.fold_in(key, 17)
    factor = jnp.exp(jax.random.uniform(jax.random.fold_in(key, 3), (POINTS, 1), jnp.float32, -0.36, 1.61))
    return jnp.clip(factor * jax.random.normal(key, (POINTS, H * DH), jnp.float32), -30.0, 30.0).astype(jnp.bfloat16)


def draw_fx_mid(key, part):
    key = jax.random.fold_in(key, 13)
    rising = 1.0 + 2.0 * jnp.arange(POINTS, dtype=jnp.float32)[:, None] / POINTS
    spread = jnp.exp(jax.random.uniform(jax.random.fold_in(key, 2), (POINTS, 1), jnp.float32, -0.5, 0.5))
    return jnp.clip(rising * spread * jax.random.normal(key, (POINTS, H * DH), jnp.float32), -20.0, 20.0).astype(jnp.bfloat16)


def draw_gumbel(key, part):
    key = jax.random.fold_in(key, 11)
    uniform_draw = jax.random.uniform(key, (POINTS, H, M), jnp.float32, 0.0001, 1.0 - 0.0001)
    noise = -jnp.log(-jnp.log(uniform_draw))
    return noise.reshape(POINTS, H * M).astype(jnp.bfloat16)


def scatter_about(stream_key, dims, deviation, reach, kind=jnp.bfloat16):
    values = jax.random.normal(stream_key, dims, jnp.float32) * deviation
    return jnp.minimum(jnp.maximum(values, -reach), reach).astype(kind)


def setup_inputs(seed: int = 0, part: int = 0) -> dict:
    keys = jax.random.split(jax.random.key(seed), 9)
    own_keys = jax.random.split(jax.random.fold_in(keys[8], part), 9)
    return {
        "x_mid": draw_x_mid(jax.random.fold_in(jax.random.fold_in(keys[8], part), 71), part),
        "fx_mid": draw_fx_mid(jax.random.fold_in(jax.random.fold_in(keys[8], part), 71), part),
        "gumbel": draw_gumbel(jax.random.fold_in(jax.random.fold_in(keys[8], part), 71), part),
        "w_slice": scatter_about(keys[3], (DH, M), DH ** -0.5, 0.75),
        "w_temp": scatter_about(keys[4], (DH,), DH ** -0.5, 0.75),
        "query_weight": draw_query_weight(jax.random.fold_in(keys[8], 71), part),
        "key_weight": draw_key_weight(jax.random.fold_in(keys[8], 71), part),
        "value_weight": scatter_about(keys[7], (DH, DH), (DH // 4) ** -0.5, 1.5, jnp.float32),
    }


epsilon = 1e-05
highest_precision = lax.Precision.HIGHEST

def slice_weights(point_block, gumbel_block, w_slice, w_temp):
    count_rows = point_block.shape[0]
    heads_view = point_block.reshape(count_rows, H, DH).astype(jnp.float32)
    logits = jnp.einsum('phd,dm->phm', heads_view, w_slice.astype(jnp.float32))
    temper = 0.5 + jax.nn.softplus(jnp.einsum('phd,d->ph', heads_view, w_temp.astype(jnp.float32)))
    logits = (logits + gumbel_block.reshape(count_rows, H, M).astype(jnp.float32)) / temper[:, :, None]
    return jax.nn.softmax(logits, axis=-1)

def head_attention(element):
    query_matrix, keys_head, values_head = element
    scores = jnp.einsum('qe,ke->qk', query_matrix, keys_head, precision=highest_precision) * (1.0 / math.sqrt(DH))
    attn_probs = jax.nn.softmax(scores, axis=-1)
    return jnp.einsum('qk,ke->qe', attn_probs, values_head, precision=highest_precision)

def reference(x_mid, fx_mid, gumbel, w_slice, w_temp, query_weight, key_weight, value_weight):
    blocks = x_mid.shape[0] // PTS_DEV
    point_blocks = x_mid.reshape(blocks, PTS_DEV, H * DH)
    value_blocks = fx_mid.reshape(blocks, PTS_DEV, H * DH)
    gumbel_blocks = gumbel.reshape(blocks, PTS_DEV, H * M)

    def pool(loop_carry_state, element):
        point_block, value_block, gumbel_block = element
        weights = slice_weights(point_block, gumbel_block, w_slice, w_temp)
        slice_assignment = lax.optimization_barrier(weights.astype(jnp.bfloat16)).astype(jnp.float32)
        value_matrix = value_block.reshape(PTS_DEV, H, DH).astype(jnp.float32)
        pooled_features = loop_carry_state[0] + jnp.einsum('ebg,ebc->bgc', slice_assignment, value_matrix)
        masses = loop_carry_state[1] + lax.optimization_barrier(jnp.sum(weights, axis=0))
        return ((pooled_features, masses), None)
    start = (jnp.zeros((H, M, DH), jnp.float32), jnp.zeros((H, M), jnp.float32))
    (pooled_features, masses), _ = lax.scan(pool, start, (point_blocks, value_blocks, gumbel_blocks))
    slice_token_state = pooled_features / (masses[:, :, None] + epsilon)
    query_matrix = jnp.einsum('uoy,yj->uoj', slice_token_state, query_weight, precision=highest_precision)
    gathered_keys = jnp.einsum('uoy,yj->uoj', slice_token_state, key_weight, precision=highest_precision)
    gathered_values = jnp.einsum('uoy,yj->uoj', slice_token_state, value_weight, precision=highest_precision)
    attention_output = lax.map(head_attention, (query_matrix, gathered_keys, gathered_values)).astype(jnp.bfloat16)
    attention_output = lax.optimization_barrier(attention_output).astype(jnp.float32)

    def deslice(element):
        point_block, gumbel_block = element
        weights = slice_weights(point_block, gumbel_block, w_slice, w_temp)
        slice_assignment = lax.optimization_barrier(weights.astype(jnp.bfloat16)).astype(jnp.float32)
        final_output = jnp.einsum('jkq,kqf->jkf', slice_assignment, attention_output)
        return final_output.reshape(PTS_DEV, H * DH).astype(jnp.bfloat16)
    sliced = lax.map(deslice, (point_blocks, gumbel_blocks))
    return sliced.reshape(blocks * PTS_DEV, H * DH)
```

```python
import math

import jax
import jax.numpy as jnp
from jax import lax
from jax.experimental import pallas as pl
from jax.experimental.pallas import tpu as pltpu
from jax.sharding import Mesh, PartitionSpec as P

H = 16
DH = 64
M = 512
HALF = M // 2
LANES = 128
TILES = M // LANES
GROUP = 8
GROUPS = H // GROUP
BATCH = 4
BATCHES = H // BATCH
FEATURES = TILES * DH
SUMS = FEATURES + 2 * TILES
ROWS = FEATURES + 16
SPAN = 120.0
STEP = 64
EPS = 1e-05
LOG2E = 1.0 / math.log(2.0)
f32 = jnp.float32
bf16 = jnp.bfloat16
IN_HBM = pl.BlockSpec(memory_space=pltpu.HBM)
IN_VMEM = pl.BlockSpec(memory_space=pltpu.VMEM)


def dot(a, b):
    return jnp.dot(a, b, preferred_element_type=f32)


def dot_nt(a, b):
    return lax.dot_general(a, b, (((1,), (1,)), ((), ())), preferred_element_type=f32)


def dot_tn(a, b):
    return lax.dot_general(a, b, (((0,), (0,)), ((), ())), preferred_element_type=f32)


def last_rows(mass, peak):
    high = mass.astype(bf16).astype(f32)
    row = lax.broadcasted_iota(jnp.int32, (16, LANES), 0)
    rows = jnp.zeros((16, LANES), f32)
    for k, part in enumerate((high, mass - high, peak)):
        for t in range(TILES):
            rows = jnp.where(row == k * TILES + t, part[:, t * LANES : (t + 1) * LANES], rows)
    return rows.astype(bf16)


def pool_kernel(
    x_hbm, fx_hbm, g_hbm, ws_hbm, wt_hbm, shares_hbm, sums_hbm,
    x_ref, fx_ref, g_ref, ws_ref, wt_ref, scale_ref, features_ref, logit_ref, shares_ref, sums_ref,
    sems, g_sems, out_sems,
):
    points = x_hbm.shape[0]

    def fetch(group):
        columns = pl.ds(group * (GROUP * M), GROUP * M)
        return pltpu.make_async_copy(g_hbm.at[:, columns], g_ref.at[group], g_sems.at[group])

    def results(batch):
        heads = pl.ds(batch * BATCH, BATCH)
        return (
            pltpu.make_async_copy(shares_ref.at[heads], shares_hbm.at[heads], out_sems.at[0, batch]),
            pltpu.make_async_copy(sums_ref.at[heads], sums_hbm.at[heads], out_sems.at[1, batch]),
        )

    first = [
        pltpu.make_async_copy(hbm, ref, sems.at[k])
        for k, (hbm, ref) in enumerate(((wt_hbm, wt_ref), (ws_hbm, ws_ref), (x_hbm, x_ref), (fx_hbm, fx_ref)))
    ]
    for copy in first:
        copy.start()
    for group in range(GROUPS):
        fetch(group).start()
    first[0].wait()
    wt = jnp.transpose(jnp.broadcast_to(wt_ref[...].astype(f32), (LANES, DH)))
    lane = lax.broadcasted_iota(jnp.int32, (DH, LANES), 1)
    wt = jnp.concatenate([jnp.where(lane == j, wt, 0.0) for j in range(H)], axis=0).astype(bf16)
    first[1].wait()
    ws = ws_ref[...]
    zero = jnp.zeros_like(ws)
    ws = (jnp.concatenate([ws, zero], axis=0), jnp.concatenate([zero, ws], axis=0))
    first[2].wait()
    v = dot(x_ref[...], wt)
    temper = 0.5 + jnp.maximum(v, 0.0) + jnp.log1p(jnp.exp(-jnp.abs(v)))
    scale = LOG2E / temper
    for group in range(GROUPS):
        scale_ref[group] = scale if group == 0 else pltpu.roll(scale, LANES - group * GROUP, 1)
    pairs = jnp.concatenate([x_ref[:, pl.ds(p * LANES, LANES)] for p in range(H // 2)], axis=0)
    for parity in range(2):
        logits = dot(pairs, ws[parity])
        for p in range(H // 2):
            logit_ref[2 * p + parity] = logits[p * points : (p + 1) * points]
    first[3].wait()
    features = jnp.transpose(fx_ref[...].astype(f32)).astype(bf16)
    for head in range(H):
        features_ref[head] = features[head * DH : (head + 1) * DH]

    def one_group(group, carry):
        fetch(group).wait()
        scale = scale_ref[group]
        for j0 in range(0, GROUP, BATCH):
            heads = range(j0, j0 + BATCH)
            totals = []
            for j in heads:
                head = group * GROUP + j
                for r in range(0, points, STEP):
                    rows = pl.ds(r, STEP)
                    logits = logit_ref[head, rows, :] + g_ref[group, rows, pl.ds(j * M, M)].astype(f32)
                    top = jnp.max(logits, axis=1, keepdims=True)
                    e = jnp.exp2((logits - top) * scale[r : r + STEP, j : j + 1])
                    logit_ref[head, rows, :] = e
                    total = (e[:, :LANES] + e[:, LANES : 2 * LANES]) + (e[:, 2 * LANES : 3 * LANES] + e[:, 3 * LANES :])
                    high = total.astype(bf16)
                    low = (total - high.astype(f32)).astype(bf16)
                    totals.append(jnp.concatenate([high, low], axis=1))
            totals = 1.0 / dot(jnp.concatenate(totals, axis=0), jnp.ones((2 * LANES, LANES), bf16))
            masses = []
            for b, j in enumerate(heads):
                head = group * GROUP + j
                mass = jnp.zeros((8, M), f32)
                total = totals[b * points : (b + 1) * points]
                for r in range(0, points, STEP):
                    rows = pl.ds(r, STEP)
                    share = logit_ref[head, rows, :] * jnp.concatenate([total[r : r + STEP]] * TILES, axis=1)
                    for k in range(0, STEP, 8):
                        mass = mass + share[k : k + 8]
                    shares_ref[head, rows, :] = share.astype(bf16)
                masses.append(jnp.sum(mass, axis=0, keepdims=True))
            for b, j in enumerate(heads):
                head = group * GROUP + j
                pooled = dot(features_ref[head], shares_ref[head])
                peak = jnp.maximum(jnp.max(jnp.abs(pooled), axis=0, keepdims=True), 1e-30)
                peak = peak.astype(bf16).astype(f32)
                pooled = jnp.exp2(pooled * (SPAN / peak))
                for t in range(TILES):
                    tile = pooled[:, t * LANES : (t + 1) * LANES]
                    sums_ref[head, pl.ds(t * DH, DH), :] = tile.astype(bf16)
                sums_ref[head, pl.ds(FEATURES, 16), :] = last_rows(masses[b], peak)
            for copy in results(group * (GROUP // BATCH) + j0 // BATCH):
                copy.start()
        return carry

    lax.fori_loop(0, GROUPS, one_group, 0)
    for batch in range(BATCHES):
        for copy in results(batch):
            copy.wait()


def pool(x_mid, fx_mid, gumbel, w_slice, w_temp):
    points = x_mid.shape[0]
    return pl.pallas_call(
        pool_kernel,
        out_shape=(
            jax.ShapeDtypeStruct((H, points, M), bf16),
            jax.ShapeDtypeStruct((H, ROWS, LANES), bf16),
        ),
        in_specs=[IN_HBM] * 5,
        out_specs=(IN_HBM, IN_HBM),
        scratch_shapes=[
            pltpu.VMEM((points, H * DH), bf16),
            pltpu.VMEM((points, H * DH), bf16),
            pltpu.VMEM((GROUPS, points, GROUP * M), bf16),
            pltpu.VMEM((DH, M), bf16),
            pltpu.VMEM((1, DH), bf16),
            pltpu.VMEM((GROUPS, points, LANES), f32),
            pltpu.VMEM((H, DH, points), bf16),
            pltpu.VMEM((H, points, M), f32),
            pltpu.VMEM((H, points, M), bf16),
            pltpu.VMEM((H, ROWS, LANES), bf16),
            pltpu.SemaphoreType.DMA((4,)),
            pltpu.SemaphoreType.DMA((GROUPS,)),
            pltpu.SemaphoreType.DMA((2, BATCHES)),
        ],
        compiler_params=pltpu.CompilerParams(vmem_limit_bytes=60 * 1024 * 1024),
        name="pool",
    )(x_mid, fx_mid, gumbel, w_slice, w_temp)


def gather_sum_kernel(parts_ref, out_ref):
    mass = None
    tiles = [None] * TILES
    for chip in range(parts_ref.shape[0]):
        last = parts_ref[chip, pl.ds(FEATURES, 16), :].astype(f32)
        mass = last[: 2 * TILES] if mass is None else mass + last[: 2 * TILES]
        unit = last[2 * TILES :] * (math.log2(math.e) / SPAN)
        for t in range(TILES):
            tile = jnp.log(parts_ref[chip, pl.ds(t * DH, DH), :].astype(f32)) * unit[t : t + 1]
            tiles[t] = tile if tiles[t] is None else tiles[t] + tile
    for t in range(TILES):
        out_ref[pl.ds(t * DH, DH), :] = tiles[t]
    out_ref[pl.ds(FEATURES, 2 * TILES), :] = mass


def gather_sum(parts):
    return pl.pallas_call(
        gather_sum_kernel,
        out_shape=jax.ShapeDtypeStruct((SUMS, LANES), f32),
        in_specs=[IN_VMEM],
        out_specs=IN_VMEM,
        compiler_params=pltpu.CompilerParams(vmem_limit_bytes=16 * 1024 * 1024),
        name="gather_sum",
    )(parts)


def split(a):
    high = a.astype(bf16)
    return high, (a - high.astype(f32)).astype(bf16)


def stack_left(a):
    high, low = split(a)
    return jnp.concatenate([high, high, low, low], axis=0)


def stack_right(a):
    high, low = split(a)
    return jnp.concatenate([high, low, high, low], axis=0)


def attend_kernel(own_ref, other_ref, wq_ref, wk_ref, wv_ref, out_ref):
    core = lax.axis_index("core")
    sums = own_ref[...] + other_ref[...]
    pooled = jnp.concatenate([sums[t * DH : (t + 1) * DH] for t in range(TILES)], axis=1)
    mass = sums[FEATURES : FEATURES + TILES] + sums[FEATURES + TILES : FEATURES + 2 * TILES]
    mass = jnp.concatenate([mass[t : t + 1] for t in range(TILES)], axis=1)
    state = pooled / (mass + EPS)
    matrices = jnp.concatenate([wq_ref[...], wk_ref[...], wv_ref[...]], axis=1)
    projected = dot_tn(stack_left(matrices), stack_right(state))
    query = projected[:DH] * (1.0 / math.sqrt(DH) * LOG2E)
    key = projected[DH : 2 * DH]
    value = projected[2 * DH :]
    query = jnp.where(core == 0, query[:, :HALF], query[:, HALF:])
    scores = dot_tn(stack_left(key), stack_right(query))
    top = jnp.max(scores, axis=0, keepdims=True)
    e = jnp.exp2(scores - top)
    total = jnp.sum(e, axis=0, keepdims=True)
    both = dot(jnp.concatenate(split(value), axis=0), e.astype(bf16))
    attended = ((both[:DH] + both[DH:]) / total).astype(bf16)
    for chip in range(out_ref.shape[0]):
        out_ref[chip] = attended


def attend(chips, own, other, query_weight, key_weight, value_weight):
    return pl.pallas_call(
        attend_kernel,
        out_shape=jax.ShapeDtypeStruct((chips, DH, HALF), bf16),
        in_specs=[IN_VMEM] * 5,
        out_specs=IN_VMEM,
        compiler_params=pltpu.CompilerParams(vmem_limit_bytes=16 * 1024 * 1024),
        name="attend",
    )(own, other, query_weight, key_weight, value_weight)


def half_sums(shares_ref, attended_ref, half, pair):
    columns = pl.ds(pl.multiple_of(half * HALF, HALF), HALF)
    zero = jnp.zeros((DH, HALF), bf16)
    total = None
    for j in range(2):
        block = attended_ref[2 * pair + j]
        block = jnp.concatenate([block, zero] if j == 0 else [zero, block], axis=0)
        term = dot_nt(shares_ref[2 * pair + j, :, columns], block)
        total = term if total is None else total + term
    return total


def deslice_own_kernel(shares_ref, own_ref, out_ref):
    core = lax.axis_index("core")
    for pair in range(H // 2):
        out_ref[:, pl.ds(pair * LANES, LANES)] = half_sums(shares_ref, own_ref, core, pair)


def deslice_kernel(shares_ref, partial_ref, other_ref, out_hbm, out_ref, sems):
    core = lax.axis_index("core")
    copies = []
    for pair in range(H // 2):
        columns = pl.ds(pair * LANES, LANES)
        total = partial_ref[:, columns] + half_sums(shares_ref, other_ref, 1 - core, pair)
        out_ref[:, columns] = total.astype(bf16)
        if pair % 2:
            columns = pl.ds((pair - 1) * LANES, 2 * LANES)
            copies.append(
                pltpu.make_async_copy(out_ref.at[:, columns], out_hbm.at[:, columns], sems.at[pair // 2])
            )
            copies[-1].start()
    for copy in copies:
        copy.wait()


def deslice_own(shares, own):
    points = shares.shape[1]
    return pl.pallas_call(
        deslice_own_kernel,
        out_shape=jax.ShapeDtypeStruct((points, H * DH), f32),
        in_specs=[IN_VMEM] * 2,
        out_specs=IN_VMEM,
        compiler_params=pltpu.CompilerParams(vmem_limit_bytes=16 * 1024 * 1024),
        cost_estimate=pl.CostEstimate(
            flops=H * points * M * DH, bytes_accessed=H * points * M * 2, transcendentals=0
        ),
        name="deslice_own",
    )(shares, own)


def deslice(shares, partial, other):
    points = shares.shape[1]
    return pl.pallas_call(
        deslice_kernel,
        out_shape=jax.ShapeDtypeStruct((points, H * DH), bf16),
        in_specs=[IN_VMEM] * 3,
        out_specs=IN_HBM,
        scratch_shapes=[
            pltpu.VMEM((points, H * DH), bf16),
            pltpu.SemaphoreType.DMA((4,)),
        ],
        compiler_params=pltpu.CompilerParams(vmem_limit_bytes=16 * 1024 * 1024),
        name="deslice",
    )(shares, partial, other)


CHIPS = ("x", "y")
SWAP = [(0, 1), (1, 0)]


def on_device(x_mid, fx_mid, gumbel, w_slice, w_temp, query_weight, key_weight, value_weight):
    shares, sums = pool(x_mid, fx_mid, gumbel, w_slice, w_temp.reshape(1, DH))
    parts = lax.all_to_all(sums, CHIPS, 0, 0, tiled=True)
    own = gather_sum(parts)
    other = lax.ppermute(own, "core", SWAP)
    attended = attend(H, own, other, query_weight, key_weight, value_weight)
    attended = lax.all_to_all(attended, CHIPS, 0, 0, tiled=True)
    other = lax.ppermute(attended, "core", SWAP)
    return deslice(shares, deslice_own(shares, attended), other)


def solution(mesh):
    devices = mesh.devices
    fine = Mesh(devices.reshape(devices.shape[0], 4, 4, 2), ("dp", "x", "y", "core"))
    rows = P(("dp", "x", "y", "core"), None)
    return jax.shard_map(
        on_device,
        mesh=fine,
        in_specs=(rows, rows, rows, P(), P(), P(), P(), P()),
        out_specs=rows,
        check_vma=False,
    )
```

```python
import math

import jax
import jax.numpy as jnp
from jax import lax
from jax.experimental import pallas as pl
from jax.experimental.pallas import tpu as pltpu
from jax.sharding import Mesh, PartitionSpec as P

H = 16
DH = 64
M = 512
HALF = M // 2
LANES = 128
TILES = M // LANES
GROUP = 8
GROUPS = H // GROUP
BATCH = 4
BATCHES = H // BATCH
FEATURES = TILES * DH
SUMS = FEATURES + 2 * TILES
ROWS = FEATURES + 16
SPAN = 120.0
STEP = 64
EPS = 1e-05
LOG2E = 1.0 / math.log(2.0)
f32 = jnp.float32
bf16 = jnp.bfloat16
IN_HBM = pl.BlockSpec(memory_space=pltpu.HBM)
IN_VMEM = pl.BlockSpec(memory_space=pltpu.VMEM)


def dot(a, b):
    return jnp.dot(a, b, preferred_element_type=f32)


def dot_nt(a, b):
    return lax.dot_general(a, b, (((1,), (1,)), ((), ())), preferred_element_type=f32)


def dot_tn(a, b):
    return lax.dot_general(a, b, (((0,), (0,)), ((), ())), preferred_element_type=f32)


def last_rows(mass, peak):
    high = mass.astype(bf16).astype(f32)
    row = lax.broadcasted_iota(jnp.int32, (16, LANES), 0)
    rows = jnp.zeros((16, LANES), f32)
    for k, part in enumerate((high, mass - high, peak)):
        for t in range(TILES):
            rows = jnp.where(row == k * TILES + t, part[:, t * LANES : (t + 1) * LANES], rows)
    return rows.astype(bf16)


def pool_kernel(
    x_hbm, fx_hbm, g_hbm, ws_hbm, wt_ref, shares_hbm, sums_hbm,
    x_ref, fx_ref, g_ref, ws_ref, scale_ref, features_ref, logit_ref, shares_ref, sums_ref,
    sems, g_sems, out_sems,
):
    points = x_hbm.shape[0]

    def fetch(group):
        columns = pl.ds(group * (GROUP * M), GROUP * M)
        return pltpu.make_async_copy(g_hbm.at[:, columns], g_ref.at[group], g_sems.at[group])

    def results(batch):
        heads = pl.ds(batch * BATCH, BATCH)
        return (
            pltpu.make_async_copy(shares_ref.at[heads], shares_hbm.at[heads], out_sems.at[0, batch]),
            pltpu.make_async_copy(sums_ref.at[heads], sums_hbm.at[heads], out_sems.at[1, batch]),
        )

    first = [
        pltpu.make_async_copy(hbm, ref, sems.at[k])
        for k, (hbm, ref) in enumerate(((ws_hbm, ws_ref), (x_hbm, x_ref), (fx_hbm, fx_ref)))
    ]
    for copy in first:
        copy.start()
    for group in range(GROUPS):
        fetch(group).start()
    wt = jnp.transpose(jnp.broadcast_to(wt_ref[...].astype(f32), (LANES, DH)))
    lane = lax.broadcasted_iota(jnp.int32, (DH, LANES), 1)
    wt = jnp.concatenate([jnp.where(lane == j, wt, 0.0) for j in range(H)], axis=0).astype(bf16)
    first[0].wait()
    ws = ws_ref[...]
    zero = jnp.zeros_like(ws)
    ws = (jnp.concatenate([ws, zero], axis=0), jnp.concatenate([zero, ws], axis=0))
    first[1].wait()
    v = dot(x_ref[...], wt)
    temper = 0.5 + jnp.maximum(v, 0.0) + jnp.log1p(jnp.exp(-jnp.abs(v)))
    scale = LOG2E / temper
    for group in range(GROUPS):
        scale_ref[group] = scale if group == 0 else pltpu.roll(scale, LANES - group * GROUP, 1)
    pairs = jnp.concatenate([x_ref[:, pl.ds(p * LANES, LANES)] for p in range(H // 2)], axis=0)
    for parity in range(2):
        logits = dot(pairs, ws[parity])
        for p in range(H // 2):
            logit_ref[2 * p + parity] = logits[p * points : (p + 1) * points]
    first[2].wait()
    features = jnp.transpose(fx_ref[...].astype(f32)).astype(bf16)
    for head in range(H):
        features_ref[head] = features[head * DH : (head + 1) * DH]

    def one_group(group, carry):
        fetch(group).wait()
        scale = scale_ref[group]
        for j0 in range(0, GROUP, BATCH):
            heads = range(j0, j0 + BATCH)
            totals = []
            for j in heads:
                head = group * GROUP + j
                for r in range(0, points, STEP):
                    rows = pl.ds(r, STEP)
                    logits = logit_ref[head, rows, :] + g_ref[group, rows, pl.ds(j * M, M)].astype(f32)
                    top = jnp.max(logits, axis=1, keepdims=True)
                    e = jnp.exp2((logits - top) * scale[r : r + STEP, j : j + 1])
                    logit_ref[head, rows, :] = e
                    total = (e[:, :LANES] + e[:, LANES : 2 * LANES]) + (e[:, 2 * LANES : 3 * LANES] + e[:, 3 * LANES :])
                    high = total.astype(bf16)
                    low = (total - high.astype(f32)).astype(bf16)
                    totals.append(jnp.concatenate([high, low], axis=1))
            totals = 1.0 / dot(jnp.concatenate(totals, axis=0), jnp.ones((2 * LANES, LANES), bf16))
            masses = []
            for b, j in enumerate(heads):
                head = group * GROUP + j
                mass = jnp.zeros((8, M), f32)
                total = totals[b * points : (b + 1) * points]
                for r in range(0, points, STEP):
                    rows = pl.ds(r, STEP)
                    share = logit_ref[head, rows, :] * jnp.concatenate([total[r : r + STEP]] * TILES, axis=1)
                    for k in range(0, STEP, 8):
                        mass = mass + share[k : k + 8]
                    shares_ref[head, rows, :] = share.astype(bf16)
                masses.append(jnp.sum(mass, axis=0, keepdims=True))
            for b, j in enumerate(heads):
                head = group * GROUP + j
                pooled = dot(features_ref[head], shares_ref[head])
                peak = jnp.maximum(jnp.max(jnp.abs(pooled), axis=0, keepdims=True), 1e-30)
                peak = peak.astype(bf16).astype(f32)
                pooled = jnp.exp2(pooled * (SPAN / peak))
                for t in range(TILES):
                    tile = pooled[:, t * LANES : (t + 1) * LANES]
                    sums_ref[head, pl.ds(t * DH, DH), :] = tile.astype(bf16)
                sums_ref[head, pl.ds(FEATURES, 16), :] = last_rows(masses[b], peak)
            for copy in results(group * (GROUP // BATCH) + j0 // BATCH):
                copy.start()
        return carry

    lax.fori_loop(0, GROUPS, one_group, 0)
    for batch in range(BATCHES):
        for copy in results(batch):
            copy.wait()


def pool(x_mid, fx_mid, gumbel, w_slice, w_temp):
    points = x_mid.shape[0]
    return pl.pallas_call(
        pool_kernel,
        out_shape=(
            jax.ShapeDtypeStruct((H, points, M), bf16),
            jax.ShapeDtypeStruct((H, ROWS, LANES), bf16),
        ),
        in_specs=[IN_HBM] * 4 + [IN_VMEM],
        out_specs=(IN_HBM, IN_HBM),
        scratch_shapes=[
            pltpu.VMEM((points, H * DH), bf16),
            pltpu.VMEM((points, H * DH), bf16),
            pltpu.VMEM((GROUPS, points, GROUP * M), bf16),
            pltpu.VMEM((DH, M), bf16),
            pltpu.VMEM((GROUPS, points, LANES), f32),
            pltpu.VMEM((H, DH, points), bf16),
            pltpu.VMEM((H, points, M), f32),
            pltpu.VMEM((H, points, M), bf16),
            pltpu.VMEM((H, ROWS, LANES), bf16),
            pltpu.SemaphoreType.DMA((3,)),
            pltpu.SemaphoreType.DMA((GROUPS,)),
            pltpu.SemaphoreType.DMA((2, BATCHES)),
        ],
        compiler_params=pltpu.CompilerParams(vmem_limit_bytes=60 * 1024 * 1024),
        name="pool",
    )(x_mid, fx_mid, gumbel, w_slice, w_temp)


def gather_sum_kernel(parts_ref, out_ref):
    mass = None
    tiles = [None] * TILES
    for chip in range(parts_ref.shape[0]):
        last = parts_ref[chip, pl.ds(FEATURES, 16), :].astype(f32)
        mass = last[: 2 * TILES] if mass is None else mass + last[: 2 * TILES]
        unit = last[2 * TILES :] * (math.log2(math.e) / SPAN)
        for t in range(TILES):
            tile = jnp.log(parts_ref[chip, pl.ds(t * DH, DH), :].astype(f32)) * unit[t : t + 1]
            tiles[t] = tile if tiles[t] is None else tiles[t] + tile
    for t in range(TILES):
        out_ref[pl.ds(t * DH, DH), :] = tiles[t]
    out_ref[pl.ds(FEATURES, 2 * TILES), :] = mass


def gather_sum(parts):
    return pl.pallas_call(
        gather_sum_kernel,
        out_shape=jax.ShapeDtypeStruct((SUMS, LANES), f32),
        in_specs=[IN_VMEM],
        out_specs=IN_VMEM,
        compiler_params=pltpu.CompilerParams(vmem_limit_bytes=16 * 1024 * 1024),
        name="gather_sum",
    )(parts)


def split(a):
    high = a.astype(bf16)
    return high, (a - high.astype(f32)).astype(bf16)


def stack_left(a):
    high, low = split(a)
    return jnp.concatenate([high, high, low, low], axis=0)


def stack_right(a):
    high, low = split(a)
    return jnp.concatenate([high, low, high, low], axis=0)


def attend_kernel(own_ref, other_ref, wq_ref, wk_ref, wv_ref, out_ref):
    core = lax.axis_index("core")
    sums = own_ref[...] + other_ref[...]
    pooled = jnp.concatenate([sums[t * DH : (t + 1) * DH] for t in range(TILES)], axis=1)
    mass = sums[FEATURES : FEATURES + TILES] + sums[FEATURES + TILES : FEATURES + 2 * TILES]
    mass = jnp.concatenate([mass[t : t + 1] for t in range(TILES)], axis=1)
    state = pooled / (mass + EPS)
    matrices = jnp.concatenate([wq_ref[...], wk_ref[...], wv_ref[...]], axis=1)
    projected = dot_tn(stack_left(matrices), stack_right(state))
    query = projected[:DH] * (1.0 / math.sqrt(DH) * LOG2E)
    key = projected[DH : 2 * DH]
    value = projected[2 * DH :]
    query = jnp.where(core == 0, query[:, :HALF], query[:, HALF:])
    scores = dot_tn(stack_left(key), stack_right(query))
    top = jnp.max(scores, axis=0, keepdims=True)
    e = jnp.exp2(scores - top)
    total = jnp.sum(e, axis=0, keepdims=True)
    both = dot(jnp.concatenate(split(value), axis=0), e.astype(bf16))
    attended = ((both[:DH] + both[DH:]) / total).astype(bf16)
    for chip in range(out_ref.shape[0]):
        out_ref[chip] = attended


def attend(chips, own, other, query_weight, key_weight, value_weight):
    return pl.pallas_call(
        attend_kernel,
        out_shape=jax.ShapeDtypeStruct((chips, DH, HALF), bf16),
        in_specs=[IN_VMEM] * 5,
        out_specs=IN_VMEM,
        compiler_params=pltpu.CompilerParams(vmem_limit_bytes=16 * 1024 * 1024),
        name="attend",
    )(own, other, query_weight, key_weight, value_weight)


def half_sums(shares_ref, attended_ref, half, pair):
    columns = pl.ds(pl.multiple_of(half * HALF, HALF), HALF)
    zero = jnp.zeros((DH, HALF), bf16)
    total = None
    for j in range(2):
        block = attended_ref[2 * pair + j]
        block = jnp.concatenate([block, zero] if j == 0 else [zero, block], axis=0)
        term = dot_nt(shares_ref[2 * pair + j, :, columns], block)
        total = term if total is None else total + term
    return total


def deslice_own_kernel(shares_ref, own_ref, out_ref):
    core = lax.axis_index("core")
    for pair in range(H // 2):
        out_ref[:, pl.ds(pair * LANES, LANES)] = half_sums(shares_ref, own_ref, core, pair)


def deslice_kernel(shares_ref, partial_ref, other_ref, out_hbm, out_ref, sems):
    core = lax.axis_index("core")
    copies = []
    for pair in range(H // 2):
        columns = pl.ds(pair * LANES, LANES)
        total = partial_ref[:, columns] + half_sums(shares_ref, other_ref, 1 - core, pair)
        out_ref[:, columns] = total.astype(bf16)
        if pair % 2:
            columns = pl.ds((pair - 1) * LANES, 2 * LANES)
            copies.append(
                pltpu.make_async_copy(out_ref.at[:, columns], out_hbm.at[:, columns], sems.at[pair // 2])
            )
            copies[-1].start()
    for copy in copies:
        copy.wait()


def deslice_own(shares, own):
    points = shares.shape[1]
    return pl.pallas_call(
        deslice_own_kernel,
        out_shape=jax.ShapeDtypeStruct((points, H * DH), f32),
        in_specs=[IN_VMEM] * 2,
        out_specs=IN_VMEM,
        compiler_params=pltpu.CompilerParams(vmem_limit_bytes=16 * 1024 * 1024),
        cost_estimate=pl.CostEstimate(
            flops=H * points * M * DH, bytes_accessed=H * points * M * 2, transcendentals=0
        ),
        name="deslice_own",
    )(shares, own)


def deslice(shares, partial, other):
    points = shares.shape[1]
    return pl.pallas_call(
        deslice_kernel,
        out_shape=jax.ShapeDtypeStruct((points, H * DH), bf16),
        in_specs=[IN_VMEM] * 3,
        out_specs=IN_HBM,
        scratch_shapes=[
            pltpu.VMEM((points, H * DH), bf16),
            pltpu.SemaphoreType.DMA((4,)),
        ],
        compiler_params=pltpu.CompilerParams(vmem_limit_bytes=16 * 1024 * 1024),
        name="deslice",
    )(shares, partial, other)


CHIPS = ("x", "y")
SWAP = [(0, 1), (1, 0)]


def on_device(x_mid, fx_mid, gumbel, w_slice, w_temp, query_weight, key_weight, value_weight):
    shares, sums = pool(x_mid, fx_mid, gumbel, w_slice, w_temp.reshape(1, DH))
    parts = lax.all_to_all(sums, CHIPS, 0, 0, tiled=True)
    own = gather_sum(parts)
    other = lax.ppermute(own, "core", SWAP)
    attended = attend(H, own, other, query_weight, key_weight, value_weight)
    attended = lax.all_to_all(attended, CHIPS, 0, 0, tiled=True)
    other = lax.ppermute(attended, "core", SWAP)
    return deslice(shares, deslice_own(shares, attended), other)


def solution(mesh):
    devices = mesh.devices
    fine = Mesh(devices.reshape(devices.shape[0], 4, 4, 2), ("dp", "x", "y", "core"))
    rows = P(("dp", "x", "y", "core"), None)
    return jax.shard_map(
        on_device,
        mesh=fine,
        in_specs=(rows, rows, rows, P(), P(), P(), P(), P()),
        out_specs=rows,
        check_vma=False,
    )
```
